32 devices in a mesh: groups: 2 (over x), replica: 8 (over z, y), tensor: 2 (over core).
Axes of the slice: x: 2, y: 2, z: 4, core: 2. Of those that a mesh axis runs over, the one named last changes fastest.
Arguments:
- tokens: bfloat16 [12288, 4096], P(('groups', 'replica'), 'tensor'), parts along dimension 0, may hold values from -6 to 6
- query_matrix: bfloat16 [4096, 4096], P('replica', 'tensor'), may hold values from -0.09375 to 0.09375
- adapter_down_weight: bfloat16 [128, 4096, 64], P(('groups', 'replica'), 'tensor'), parts along dimension 0, may hold values from -0.09375 to 0.09375
- adapter_up_weight: bfloat16 [128, 64, 4096], P(('groups', 'replica'), None, 'tensor'), parts along dimension 0, may hold values from -0.75 to 0.75
- block_adapter_ids: int32 [96], P(('groups', 'replica')), parts along dimension 0, may hold values from 0 to 63, as said below
- block_live_rows: int32 [96], P(('groups', 'replica')), parts along dimension 0, may hold values from 1 to 128, as said below
Outputs:
- queries: bfloat16 [12288, 4096], P(('groups', 'replica'), 'tensor'), parts along dimension 0
The draws below stay inside these ranges and needn't reach their ends.
There are 2 independent parts, one for each index of `groups`. The reference program is written for one: setup_inputs(seed, part) draws one part's arguments, and reference() takes and returns one part's arrays. A program takes and returns all parts, laid end to end along the dimension named above; an argument that names none is the same for every part. Nothing has to cross between parts.
Inputs may be any that keep to these rules, and one draw needn't show every extreme that they name: `block_adapter_ids`: adapter a is owned by replica index a // 8. A block on replica index r uses an adapter owned by index r - 1, r or r + 1 (modulo the replica axis), and every replica index has at least one block of each neighbour's adapters. `block_live_rows`: every replica index has at least one full block.
All inputs are finite; a program needn't handle non-finite values.
Results may differ from the reference program's by a relative error of at most 0.0047.
Values may be sent and summed in bfloat16 or wider, within the bound.
No kernel may reach another device: no remote copies, remote signals or barrier semaphores. Data moves between devices by JAX's collectives and lax.ppermute only.
A program may use at most 128 MiB of HBM per device.

```python
import jax
import jax.numpy as jnp
from jax import lax

MODEL_WIDTH = 4096
ADAPTER_RANK = 64
BLOCK = 128
ADP_DEV = 8
BLK_DEV = 6
ADAPTER_TOTAL = 64
NBLK = 48
TOKEN_TOTAL = 6144


def draw_block_adapter_ids(key, part):
    key = jax.random.fold_in(key, 11)
    cycle_count = NBLK // BLK_DEV
    keys = jax.random.split(key, 4)

    def permute_one(single_key):
        return jax.random.permutation(single_key, BLK_DEV)
    orders = jax.vmap(permute_one)(jax.random.split(keys[0], cycle_count))
    slot_rank = jnp.argsort(orders, axis=1)
    offsets = jax.random.randint(keys[1], (cycle_count, BLK_DEV), -1, 2)
    offsets = jnp.where(slot_rank == 0, -1, jnp.where(slot_rank == 1, 1, offsets))
    owner_dev = (jnp.arange(cycle_count)[:, None] + offsets) % cycle_count
    first_pick = jax.random.randint(keys[2], (cycle_count, BLK_DEV), 0, ADP_DEV)
    second_pick = jax.random.randint(keys[3], (cycle_count, BLK_DEV), 0, ADP_DEV)
    local_index = jnp.minimum(first_pick, second_pick)
    return (owner_dev * ADP_DEV + local_index).reshape(NBLK).astype(jnp.int32)


def draw_block_live_rows(key, part):
    key = jax.random.fold_in(key, 23)
    cycle_count = NBLK // BLK_DEV
    keys = jax.random.split(key, 2)
    counts = jax.random.randint(keys[0], (cycle_count, BLK_DEV), 1, BLOCK + 1)
    full_slot = jax.random.randint(keys[1], (cycle_count, 1), 0, BLK_DEV)
    counts = jnp.where(jnp.arange(BLK_DEV)[None, :] == full_slot, BLOCK, counts)
    return counts.reshape(NBLK).astype(jnp.int32)


def levels(stream_key, shape, shards, smallest, top_value):
    def one(axis_at, blocks):
        draws = jax.random.uniform(jax.random.fold_in(jax.random.fold_in(stream_key, 6), axis_at), (blocks,), jnp.float32, smallest / len(shards), top_value / len(shards))
        return jnp.repeat(jnp.exp(draws), shape[axis_at] // blocks).reshape((-1,) + (1,) * (len(shape) - axis_at - 1))

    gain = one(*shards[0])
    for cut in shards[1:]:
        gain = gain * one(*cut)
    return gain


def noise(key, dims, deviation, most, cuts=(), held_as=jnp.bfloat16):
    result = jax.random.normal(key, dims, jnp.float32) * deviation
    if len(cuts) > 0:
        result = levels(key, dims, cuts, -0.22, 0.18) * result
    return jnp.clip(result, min=-most, max=most).astype(held_as)


def setup_inputs(seed: int = 0, part: int = 0) -> dict:
    seeds = jax.random.split(jax.random.key(seed), 7)
    part_keys = jax.random.split(jax.random.fold_in(seeds[6], part), 7)
    tokens = noise(part_keys[0], (TOKEN_TOTAL, MODEL_WIDTH), 1.0, 6.0, ((0, 8), (1, 2)))
    query_matrix = noise(seeds[1], (MODEL_WIDTH, MODEL_WIDTH), MODEL_WIDTH ** -0.5, 0.09375, ((0, 8), (1, 2)))
    adapter_down_weight = noise(part_keys[2], (ADAPTER_TOTAL, MODEL_WIDTH, ADAPTER_RANK), MODEL_WIDTH ** -0.5, 0.09375, ((0, 8), (1, 2)))
    adapter_up_weight = noise(part_keys[3], (ADAPTER_TOTAL, ADAPTER_RANK, MODEL_WIDTH), ADAPTER_RANK ** -0.5, 0.75, ((0, 8), (2, 2)))
    block_adapter_ids = draw_block_adapter_ids(jax.random.fold_in(jax.random.fold_in(seeds[6], part), 71), part)
    block_live_rows = draw_block_live_rows(jax.random.fold_in(jax.random.fold_in(seeds[6], part), 71), part)
    return dict(tokens=tokens, query_matrix=query_matrix, adapter_down_weight=adapter_down_weight, adapter_up_weight=adapter_up_weight, block_adapter_ids=block_adapter_ids, block_live_rows=block_live_rows)


adapter_scale = 2.0


def reference(tokens, query_matrix, adapter_down_weight, adapter_up_weight, block_adapter_ids, block_live_rows):
    base_output = jnp.dot(tokens, query_matrix, preferred_element_type=jnp.float32)
    token_block_list = tokens.reshape(NBLK, BLOCK, MODEL_WIDTH)

    def single_block(inputs):
        block_token_rows, adapter_entry = inputs
        low_rank_state = jnp.dot(block_token_rows, adapter_down_weight[adapter_entry], preferred_element_type=jnp.float32).astype(jnp.bfloat16)
        return jnp.dot(low_rank_state, adapter_up_weight[adapter_entry], preferred_element_type=jnp.float32)

    adapter_delta = lax.map(single_block, (token_block_list, block_adapter_ids)).reshape(TOKEN_TOTAL, MODEL_WIDTH)
    live_row_count = (jnp.arange(BLOCK)[None, :] < block_live_rows[:, None]).reshape(TOKEN_TOTAL, 1)
    return jnp.where(live_row_count, base_output + adapter_scale * adapter_delta, 0.0).astype(jnp.bfloat16)
```

```python
import functools

import jax
import jax.numpy as jnp
import numpy as np
from jax import lax
from jax.experimental import pallas as pl
from jax.experimental.pallas import tpu as pltpu
from jax.sharding import PartitionSpec as P

ADAPTER_SCALE = 2.0
F32 = jnp.float32
VMEM_LIMIT = 48 * 1024 * 1024


def routes(count):
    planes = count // 2
    ring = [2 * z for z in range(planes)] + [2 * z + 1 for z in reversed(range(planes))]
    ahead = [(ring[p], ring[(p + 1) % count]) for p in range(count)]
    back = [(b, a) for a, b in ahead]
    across = [(i, i ^ 1) for i in range(count)]
    diagonal = [(i, (i + 1 if i % 2 else i - 1) % count) for i in range(count)]
    lift = [(i, (i + 2 if i % 2 else i - 2) % count) for i in range(count)]
    return ring, ahead, back, across, diagonal, lift


def params(count):
    return pltpu.CompilerParams(
        dimension_semantics=("arbitrary",) * count, vmem_limit_bytes=VMEM_LIMIT
    )


def pick(index, down_t, up):
    count = index.shape[0]
    block = (1,) + down_t.shape[1:]
    spec = pl.BlockSpec(block, lambda i, at: (at[i], 0, 0))
    out = pl.BlockSpec(block, lambda i, at: (i, 0, 0))

    def body(at, a, b, c, d):
        c[...] = a[...]
        d[...] = b[...]

    shape = jax.ShapeDtypeStruct((count,) + down_t.shape[1:], down_t.dtype)
    size = count * int(np.prod(block)) * 8
    return pl.pallas_call(
        body,
        grid_spec=pltpu.PrefetchScalarGridSpec(
            num_scalar_prefetch=1, grid=(count,), in_specs=[spec, spec], out_specs=[out, out]
        ),
        out_shape=[shape, shape],
        compiler_params=params(1),
        cost_estimate=pl.CostEstimate(flops=0, bytes_accessed=size, transcendentals=0),
    )(index, down_t, up)


def pick_two(which, first, second, a, b):
    count = which.shape[0]
    block = (1,) + a.shape[1:]

    def body(which_ref, first_ref, second_ref, a_ref, b_ref, out_ref):
        side = which_ref[pl.program_id(0)]

        @pl.when(side == 0)
        def _():
            out_ref[...] = a_ref[...]

        @pl.when(side != 0)
        def _():
            out_ref[...] = b_ref[...]

    return pl.pallas_call(
        body,
        grid_spec=pltpu.PrefetchScalarGridSpec(
            num_scalar_prefetch=3,
            grid=(count,),
            in_specs=[
                pl.BlockSpec(block, lambda i, w, f, s: (f[i], 0, 0)),
                pl.BlockSpec(block, lambda i, w, f, s: (s[i], 0, 0)),
            ],
            out_specs=pl.BlockSpec(block, lambda i, w, f, s: (i, 0, 0)),
        ),
        out_shape=jax.ShapeDtypeStruct((count,) + a.shape[1:], a.dtype),
        compiler_params=params(1),
        cost_estimate=pl.CostEstimate(
            flops=0, bytes_accessed=count * int(np.prod(block)) * 6, transcendentals=0
        ),
    )(which, first, second, a, b)


def choose_specs(shape, prefetched):
    block = (1,) + shape[1:]
    return [
        pl.BlockSpec(block, lambda i, table, *rest, n=n: (table[n, i], 0, 0)) for n in (1, 2)
    ]


def low_partial(table, tokens, sources):
    blocks = table.shape[1]
    rows, width = tokens.shape[0] // blocks, tokens.shape[1]
    rank = sources[0].shape[1]

    def body(table_ref, x_ref, own_ref, sent_ref, out_ref):
        place = table_ref[0, pl.program_id(0)]
        for n, ref in enumerate((own_ref, sent_ref)):

            @pl.when(place == n)
            def _(ref=ref):
                out_ref[...] = lax.dot_general(
                    x_ref[...], ref[0], (((1,), (1,)), ((), ())), preferred_element_type=F32
                )

    return pl.pallas_call(
        body,
        grid_spec=pltpu.PrefetchScalarGridSpec(
            num_scalar_prefetch=1,
            grid=(blocks,),
            in_specs=[pl.BlockSpec((rows, width), lambda i, s: (i, 0))]
            + choose_specs(sources[0].shape, 1),
            out_specs=pl.BlockSpec((rows, rank), lambda i, s: (i, 0)),
        ),
        out_shape=jax.ShapeDtypeStruct((tokens.shape[0], rank), F32),
        compiler_params=params(1),
        cost_estimate=pl.CostEstimate(
            flops=2 * tokens.shape[0] * width * rank,
            bytes_accessed=tokens.size * 2 + 8 * rank * width * 2,
            transcendentals=0,
        ),
    )(table, tokens, *sources)


def product(tokens, shards, pieces, out_type):
    rows, width = tokens.shape
    columns = pieces[0].shape[1]
    tile = 256 if rows % 256 == 0 else rows
    count = len(pieces)

    def body(at, x_ref, *refs):
        total = None
        depth = pieces[0].shape[0]
        for k in range(count):
            x = x_ref[:, pl.ds(pl.multiple_of(at[k], depth), depth)]
            if k == count - 2:
                x = x[:, : depth // 2]
            if k == count - 1:
                x = x[:, depth // 2 :]
            term = jnp.dot(x, refs[k][...], preferred_element_type=F32)
            total = term if total is None else total + term
        refs[count][...] = total.astype(out_type)

    return pl.pallas_call(
        body,
        grid_spec=pltpu.PrefetchScalarGridSpec(
            num_scalar_prefetch=1,
            grid=(rows // tile,),
            in_specs=[pl.BlockSpec((tile, width), lambda i, at: (i, 0))]
            + [pl.BlockSpec(p.shape, lambda i, at: (0, 0)) for p in pieces],
            out_specs=pl.BlockSpec((tile, columns), lambda i, at: (i, 0)),
        ),
        out_shape=jax.ShapeDtypeStruct((rows, columns), out_type),
        compiler_params=params(1),
        cost_estimate=pl.CostEstimate(
            flops=2 * rows * width * columns,
            bytes_accessed=(rows * width + width * columns + 2 * rows * columns) * 2,
            transcendentals=0,
        ),
    )(shards, tokens, *pieces)


def finish(table, live, half, low_a, low_b, mine, theirs, sources):
    blocks = table.shape[1]
    rows = mine[0].shape[0] // blocks
    widths = [m.shape[1] for m in mine]
    part = sum(widths)
    rank = sources[0].shape[1]
    chunks = len(mine)

    def body(table_ref, live_ref, half_ref, la, lb, *refs):
        out_ref = refs[-1]
        block = pl.program_id(0)
        place = table_ref[0, block]
        low = (la[...] + lb[...]).astype(jnp.bfloat16)

        def write(source, left, right):
            start = 0
            for ref in tuple(left) + tuple(right):
                width = ref.shape[1]
                delta = jnp.dot(
                    low, source[0, :, start : start + width], preferred_element_type=F32
                )
                total = ref[...].astype(F32) + ADAPTER_SCALE * delta
                alive = lax.broadcasted_iota(jnp.int32, (rows, width), 0) < live_ref[block]
                out_ref[:, start : start + width] = jnp.where(alive, total, 0.0).astype(
                    out_ref.dtype
                )
                start += width

        mine_refs, theirs_refs = refs[:chunks], refs[chunks : 2 * chunks]
        for n in range(2):
            for side in range(2):

                @pl.when(jnp.logical_and(place == n, half_ref[0] == side))
                def _(n=n, side=side):
                    if side == 0:
                        write(refs[2 * chunks + n], mine_refs, theirs_refs)
                    else:
                        write(refs[2 * chunks + n], theirs_refs, mine_refs)

    row = lambda width: pl.BlockSpec((rows, width), lambda i, s, l, h: (i, 0))
    return pl.pallas_call(
        body,
        grid_spec=pltpu.PrefetchScalarGridSpec(
            num_scalar_prefetch=3,
            grid=(blocks,),
            in_specs=[row(rank), row(rank)]
            + [row(w) for w in widths + widths]
            + choose_specs(sources[0].shape, 3),
            out_specs=row(2 * part),
        ),
        out_shape=jax.ShapeDtypeStruct((rows * blocks, 2 * part), jnp.bfloat16),
        compiler_params=params(1),
        cost_estimate=pl.CostEstimate(
            flops=4 * rows * blocks * part * rank,
            bytes_accessed=rows * blocks * part * 10 + 8 * rank * part * 4,
            transcendentals=0,
        ),
    )(table, live, half, low_a, low_b, *mine, *theirs, *sources)


def ranks(ids, owner_of, owner):
    hit = owner_of == owner
    return hit, jnp.cumsum(hit.astype(jnp.int32)) - hit.astype(jnp.int32)


def slots(ids, per_device, owner, count):
    hit, place = ranks(ids, ids // per_device, owner)
    at = jnp.arange(count)[:, None]
    chosen = jnp.logical_and(hit[None, :], place[None, :] == at)
    return jnp.sum(jnp.where(chosen, (ids % per_device)[None, :], 0), axis=1).astype(jnp.int32)


def local(groups, count, tokens, query_matrix, down, up, ids, live):
    ring, ahead, back, across, diagonal, lift = routes(count)
    rep = lambda a, route: lax.ppermute(a, "replica", route)
    partner = lambda a: lax.ppermute(a, "groups", [(i, i ^ 1) for i in range(groups)])
    other_core = lambda a: lax.ppermute(a, "tensor", [(0, 1), (1, 0)])

    depth, out_half = query_matrix.shape
    quarter = out_half // 2
    blocks = ids.shape[0]
    per_device = down.shape[0]
    most = blocks - 1
    half = (lax.axis_index("groups") % 2).astype(jnp.int32)
    me = lax.axis_index("replica").astype(jnp.int32)
    core = lax.axis_index("tensor")

    place = np.argsort(ring)
    offsets = np.zeros((count, count + 1), np.int32)
    for r in range(count):
        for step in range(1, count // 2 + 1):
            offsets[r, 2 * step - 1] = ring[(place[r] - step) % count] * depth
            offsets[r, 2 * step] = ring[(place[r] + step) % count] * depth
        offsets[r, 0] = r * depth
    shards = lax.dynamic_index_in_dim(jnp.asarray(offsets), me, 0, keepdims=False)

    def circulate(start, width):
        own = lax.dynamic_slice(query_matrix, (0, half * quarter + start), (depth, width))
        pieces = [own]
        low_side = high_side = own
        for step in range(1, count // 2 + 1):
            if step == count // 2:
                low_side, high_side = low_side[: depth // 2], high_side[depth // 2 :]
            low_side = rep(low_side, ahead)
            high_side = rep(high_side, back)
            pieces += [low_side, high_side]
        return pieces

    their_tokens = partner(tokens)

    def widen(part):
        swapped = other_core(part)
        return jnp.where(
            core == 0,
            jnp.concatenate([part, swapped], axis=1),
            jnp.concatenate([swapped, part], axis=1),
        )

    ids_across = rep(ids, across)
    ids_diagonal = rep(ids, diagonal)
    down_t = jnp.swapaxes(down, 1, 2)
    sent = pick(slots(ids_diagonal, per_device, me, most), down_t, up)
    feeder = jnp.where(me % 2 == 1, me - 2, me + 2) % count
    across_owner = ids_across // per_device
    _, feeder_place = ranks(ids_across, across_owner, feeder)
    from_feeder = (across_owner == feeder).astype(jnp.int32)
    own_at = jnp.where(across_owner == me, ids_across % per_device, 0).astype(jnp.int32)
    feeder_at = jnp.where(from_feeder == 1, jnp.minimum(feeder_place, most - 1), 0).astype(jnp.int32)
    foreign = (ids // per_device != me).astype(jnp.int32)
    table = jnp.stack(
        [
            foreign,
            jnp.where(foreign == 0, ids % per_device, 0).astype(jnp.int32),
            jnp.where(foreign == 1, jnp.arange(blocks, dtype=jnp.int32), 0),
        ]
    )

    def deliver(kind, owned):
        lifted = rep(sent[kind], lift)
        return [owned, rep(pick_two(from_feeder, own_at, feeder_at, owned, lifted), across)]

    downs = deliver(0, down_t)
    ups = deliver(1, up)
    low = low_partial(table, tokens, downs)
    low_other = other_core(low)

    my_rows, their_rows = widen(tokens), widen(their_tokens)
    mine, theirs, start = [], [], 0
    for width in (quarter // 2, quarter // 4, quarter // 4):
        pieces = circulate(start, width)
        theirs.append(partner(product(their_rows, shards, pieces, jnp.bfloat16)))
        mine.append(product(my_rows, shards, pieces, F32))
        start += width
    return finish(table, live, half.reshape(1), low, low_other, mine, theirs, ups)


def solution(mesh):
    in_specs = (
        P(("groups", "replica"), "tensor"),
        P("replica", "tensor"),
        P(("groups", "replica"), "tensor", None),
        P(("groups", "replica"), None, "tensor"),
        P(("groups", "replica")),
        P(("groups", "replica")),
    )
    out_specs = P(("groups", "replica"), "tensor")
    body = functools.partial(local, mesh.shape["groups"], mesh.shape["replica"])
    return jax.shard_map(body, mesh=mesh, in_specs=in_specs, out_specs=out_specs, check_vma=False)
```

```python
import functools

import jax
import jax.numpy as jnp
import numpy as np
from jax import lax
from jax.experimental import pallas as pl
from jax.experimental.pallas import tpu as pltpu
from jax.sharding import PartitionSpec as P

ADAPTER_SCALE = 2.0
F32 = jnp.float32
VMEM_LIMIT = 48 * 1024 * 1024


CUTS = 2
CHUNKS = (5, 3)
PLAN = [
    ("ring", 0),
    ("lift", 0),
    ("swap_mine", 0),
    ("ring_done", 0),
    ("swap_done", 0),
    ("ring", 0),
    ("lift_done", 0),
    ("across", 0),
    ("lift", 1),
    ("ring_done", 0),
    ("ring", 0),
    ("lift_done", 1),
    ("across_done", 0),
    ("across", 1),
    ("lift", 2),
    ("ring_done", 0),
    ("ring", 0),
    ("tokens_done", 0),
    ("swap_their", 0),
    ("ring_done", 0),
    ("ring", 1),
    ("swap_done", 1),
    ("base", 0),
    ("lift_done", 2),
    ("across_done", 1),
    ("across", 2),
    ("lift", 3),
    ("ring_done", 1),
    ("ring", 1),
    ("keep", 0),
    ("lift_done", 3),
    ("across_done", 2),
    ("across", 3),
    ("low", 0),
    ("ring_done", 1),
    ("ring", 1),
    ("base_done", 0),
    ("ring_done", 1),
    ("ring", 1),
    ("across_done", 3),
    ("ring_done", 1),
    ("base", 1),
    ("keep", 1),
]


def routes(count):
    planes = count // 2
    ring = [2 * z for z in range(planes)] + [2 * z + 1 for z in reversed(range(planes))]
    ahead = [(ring[p], ring[(p + 1) % count]) for p in range(count)]
    back = [(b, a) for a, b in ahead]
    across = [(i, i ^ 1) for i in range(count)]
    diagonal = [(i, (i + 1 if i % 2 else i - 1) % count) for i in range(count)]
    lift = [(i, (i + 2 if i % 2 else i - 2) % count) for i in range(count)]
    return ring, ahead, back, across, diagonal, lift


def params(count):
    return pltpu.CompilerParams(
        dimension_semantics=("arbitrary",) * count, vmem_limit_bytes=VMEM_LIMIT
    )


def pick(index, down_t, up, cuts):
    count = index.shape[0]
    _, rank, width = down_t.shape
    part = rank // cuts
    spec = pl.BlockSpec((1, rank, width), lambda i, at: (at[i], 0, 0))
    out = pl.BlockSpec((1, part, width), lambda i, at: (i, 0, 0))

    def body(at, a, b, *outs):
        for n, ref in enumerate(outs):
            source = a if n < cuts else b
            start = (n % cuts) * part
            ref[...] = source[:, start : start + part, :]

    shape = jax.ShapeDtypeStruct((count, part, width), down_t.dtype)
    return pl.pallas_call(
        body,
        grid_spec=pltpu.PrefetchScalarGridSpec(
            num_scalar_prefetch=1,
            grid=(count,),
            in_specs=[spec, spec],
            out_specs=[out] * (2 * cuts),
        ),
        out_shape=[shape] * (2 * cuts),
        compiler_params=params(1),
        cost_estimate=pl.CostEstimate(
            flops=0, bytes_accessed=count * rank * width * 8, transcendentals=0
        ),
    )(index, down_t, up)


def pick_two(which, first, second, a, b, cut):
    count = which.shape[0]
    block = (1,) + b.shape[1:]

    def body(which_ref, first_ref, second_ref, a_ref, b_ref, out_ref):
        side = which_ref[pl.program_id(0)]

        @pl.when(side == 0)
        def _():
            out_ref[...] = a_ref[...]

        @pl.when(side != 0)
        def _():
            out_ref[...] = b_ref[...]

    return pl.pallas_call(
        body,
        grid_spec=pltpu.PrefetchScalarGridSpec(
            num_scalar_prefetch=3,
            grid=(count,),
            in_specs=[
                pl.BlockSpec(block, lambda i, w, f, s: (f[i], cut, 0)),
                pl.BlockSpec(block, lambda i, w, f, s: (s[i], 0, 0)),
            ],
            out_specs=pl.BlockSpec(block, lambda i, w, f, s: (i, 0, 0)),
        ),
        out_shape=jax.ShapeDtypeStruct((count,) + b.shape[1:], b.dtype),
        compiler_params=params(1),
        cost_estimate=pl.CostEstimate(
            flops=0, bytes_accessed=count * int(np.prod(block)) * 6, transcendentals=0
        ),
    )(which, first, second, a, b)


def choose_specs(sources):
    owned, parts = sources
    specs = [pl.BlockSpec((1,) + owned.shape[1:], lambda i, table, *rest: (table[1, i], 0, 0))]
    for p in parts:
        specs.append(
            pl.BlockSpec((1,) + p.shape[1:], lambda i, table, *rest: (table[2, i], 0, 0))
        )
    return specs


def low_partial(table, tokens, sources):
    blocks = table.shape[1]
    rows, width = tokens.shape[0] // blocks, tokens.shape[1]
    rank = sources[0].shape[1]

    def body(table_ref, x_ref, own_ref, *refs):
        place = table_ref[0, pl.program_id(0)]
        out_ref = refs[-1]

        def write(weight):
            out_ref[...] = lax.dot_general(
                x_ref[...], weight, (((1,), (1,)), ((), ())), preferred_element_type=F32
            )

        @pl.when(place == 0)
        def _():
            write(own_ref[0])

        @pl.when(place != 0)
        def _():
            write(jnp.concatenate([r[0] for r in refs[:-1]], axis=0))

    return pl.pallas_call(
        body,
        grid_spec=pltpu.PrefetchScalarGridSpec(
            num_scalar_prefetch=1,
            grid=(blocks,),
            in_specs=[pl.BlockSpec((rows, width), lambda i, s: (i, 0))] + choose_specs(sources),
            out_specs=pl.BlockSpec((rows, rank), lambda i, s: (i, 0)),
        ),
        out_shape=jax.ShapeDtypeStruct((tokens.shape[0], rank), F32),
        compiler_params=params(1),
        cost_estimate=pl.CostEstimate(
            flops=2 * tokens.shape[0] * width * rank,
            bytes_accessed=tokens.size * 2 + 8 * rank * width * 2,
            transcendentals=0,
        ),
    )(table, tokens, sources[0], *sources[1])


def product(shards, same, swapped, pieces, out_type):
    rows, width = same.shape
    columns = pieces[0].shape[1]
    depth = pieces[0].shape[0]
    tile = 256 if rows % 256 == 0 else rows
    count = len(pieces)

    def body(at, same_ref, swapped_ref, *refs):
        x_ref = refs[-1]

        @pl.when(at[count] == 0)
        def _():
            x_ref[:, :width] = same_ref[...]
            x_ref[:, width:] = swapped_ref[...]

        @pl.when(at[count] != 0)
        def _():
            x_ref[:, :width] = swapped_ref[...]
            x_ref[:, width:] = same_ref[...]

        total = None
        for k in range(count):
            x = x_ref[:, pl.ds(pl.multiple_of(at[k], depth), depth)]
            if k == count - 2:
                x = x[:, : depth // 2]
            if k == count - 1:
                x = x[:, depth // 2 :]
            term = jnp.dot(x, refs[k][...], preferred_element_type=F32)
            total = term if total is None else total + term
        refs[count][...] = total.astype(out_type)

    return pl.pallas_call(
        body,
        grid_spec=pltpu.PrefetchScalarGridSpec(
            num_scalar_prefetch=1,
            grid=(rows // tile,),
            in_specs=[pl.BlockSpec((tile, width), lambda i, at: (i, 0))] * 2
            + [pl.BlockSpec(p.shape, lambda i, at: (0, 0)) for p in pieces],
            out_specs=pl.BlockSpec((tile, columns), lambda i, at: (i, 0)),
            scratch_shapes=[pltpu.VMEM((tile, 2 * width), same.dtype)],
        ),
        out_shape=jax.ShapeDtypeStruct((rows, columns), out_type),
        compiler_params=params(1),
        cost_estimate=pl.CostEstimate(
            flops=4 * rows * width * columns,
            bytes_accessed=(2 * rows * width + 2 * width * columns + 2 * rows * columns) * 2,
            transcendentals=0,
        ),
    )(shards, same, swapped, *pieces)


def finish(table, live, half, low_a, low_b, mine, theirs, sources):
    blocks = table.shape[1]
    rows = mine[0].shape[0] // blocks
    widths = [m.shape[1] for m in mine]
    part = sum(widths)
    rank = sources[0].shape[1]
    chunks = len(mine)

    def body(table_ref, live_ref, half_ref, la, lb, *refs):
        out_ref = refs[-1]
        block = pl.program_id(0)
        place = table_ref[0, block]
        low = (la[...] + lb[...]).astype(jnp.bfloat16)
        mine_refs, theirs_refs = refs[:chunks], refs[chunks : 2 * chunks]
        own_ref, part_refs = refs[2 * chunks], refs[2 * chunks + 1 : -1]

        def write(weight_of, left, right):
            start = 0
            for ref in tuple(left) + tuple(right):
                width = ref.shape[1]
                delta = jnp.dot(low, weight_of(start, width), preferred_element_type=F32)
                total = ref[...].astype(F32) + ADAPTER_SCALE * delta
                alive = lax.broadcasted_iota(jnp.int32, (rows, width), 0) < live_ref[block]
                out_ref[:, start : start + width] = jnp.where(alive, total, 0.0).astype(
                    out_ref.dtype
                )
                start += width

        def from_own(start, width):
            return own_ref[0, :, start : start + width]

        def from_parts(start, width):
            return jnp.concatenate([r[0, :, start : start + width] for r in part_refs], axis=0)

        for n, weight_of in enumerate((from_own, from_parts)):
            for side in range(2):

                @pl.when(jnp.logical_and(place == n, half_ref[0] == side))
                def _(weight_of=weight_of, side=side):
                    if side == 0:
                        write(weight_of, mine_refs, theirs_refs)
                    else:
                        write(weight_of, theirs_refs, mine_refs)

    row = lambda width: pl.BlockSpec((rows, width), lambda i, s, l, h: (i, 0))
    return pl.pallas_call(
        body,
        grid_spec=pltpu.PrefetchScalarGridSpec(
            num_scalar_prefetch=3,
            grid=(blocks,),
            in_specs=[row(rank), row(rank)]
            + [row(w) for w in widths + widths]
            + choose_specs(sources),
            out_specs=row(2 * part),
        ),
        out_shape=jax.ShapeDtypeStruct((rows * blocks, 2 * part), jnp.bfloat16),
        compiler_params=params(1),
        cost_estimate=pl.CostEstimate(
            flops=4 * rows * blocks * part * rank,
            bytes_accessed=rows * blocks * part * 10 + 8 * rank * part * 4,
            transcendentals=0,
        ),
    )(table, live, half, low_a, low_b, *mine, *theirs, sources[0], *sources[1])


def ranks(ids, owner_of, owner):
    hit = owner_of == owner
    return hit, jnp.cumsum(hit.astype(jnp.int32)) - hit.astype(jnp.int32)


def slots(ids, per_device, owner, count):
    hit, place = ranks(ids, ids // per_device, owner)
    at = jnp.arange(count)[:, None]
    chosen = jnp.logical_and(hit[None, :], place[None, :] == at)
    return jnp.sum(jnp.where(chosen, (ids % per_device)[None, :], 0), axis=1).astype(jnp.int32)


class Order:
    def __init__(self):
        self.last = ()

    def after(self, x):
        return lax.optimization_barrier((x,) + self.last)[0] if self.last else x

    def arrived(self, *found):
        self.last = (self.last + found)[-6:]


def local(groups, count, tokens, query_matrix, down, up, ids, live):
    ring, ahead, back, across, diagonal, lift = routes(count)
    rep = lambda a, route: lax.ppermute(a, "replica", route)
    partner = lambda a: lax.ppermute(a, "groups", [(i, i ^ 1) for i in range(groups)])
    other_core = lambda a: lax.ppermute(a, "tensor", [(0, 1), (1, 0)])
    order = Order()

    depth, out_half = query_matrix.shape
    quarter = out_half // 2
    blocks = ids.shape[0]
    per_device = down.shape[0]
    most = blocks - 1
    half = (lax.axis_index("groups") % 2).astype(jnp.int32)
    me = lax.axis_index("replica").astype(jnp.int32)
    core = lax.axis_index("tensor").astype(jnp.int32)

    place = np.argsort(ring)
    offsets = np.zeros((count, count + 1), np.int32)
    for r in range(count):
        for step in range(1, count // 2 + 1):
            offsets[r, 2 * step - 1] = ring[(place[r] - step) % count] * depth
            offsets[r, 2 * step] = ring[(place[r] + step) % count] * depth
        offsets[r, 0] = r * depth
    shards = lax.dynamic_index_in_dim(jnp.asarray(offsets), me, 0, keepdims=False)
    shards = jnp.concatenate([shards, core.reshape(1)])

    widths = [quarter * n // 8 for n in CHUNKS]
    starts = [sum(widths[:n]) for n in range(len(widths))]
    pieces = [
        [lax.dynamic_slice(query_matrix, (0, half * quarter + s), (depth, w))]
        for s, w in zip(starts, widths)
    ]

    def ring_step(chunk):
        held = pieces[chunk]
        step = (len(held) + 1) // 2
        low_side, high_side = (held[0], held[0]) if step == 1 else held[-2:]
        if step == count // 2:
            low_side, high_side = low_side[: depth // 2], high_side[depth // 2 :]
        held += [rep(order.after(low_side), ahead), rep(order.after(high_side), back)]

    their_same = partner(tokens)
    ids_across = rep(ids, across)
    ids_diagonal = rep(ids, diagonal)

    down_t = jnp.swapaxes(down, 1, 2)
    parts = pick(slots(ids_diagonal, per_device, me, most), down_t, up, CUTS)
    feeder = jnp.where(me % 2 == 1, me - 2, me + 2) % count
    across_owner = ids_across // per_device
    _, feeder_place = ranks(ids_across, across_owner, feeder)
    from_feeder = (across_owner == feeder).astype(jnp.int32)
    own_at = jnp.where(across_owner == me, ids_across % per_device, 0).astype(jnp.int32)
    feeder_at = jnp.where(from_feeder == 1, jnp.minimum(feeder_place, most - 1), 0).astype(jnp.int32)
    foreign = (ids // per_device != me).astype(jnp.int32)
    table = jnp.stack(
        [
            foreign,
            jnp.where(foreign == 0, ids % per_device, 0).astype(jnp.int32),
            jnp.where(foreign == 1, jnp.arange(blocks, dtype=jnp.int32), 0),
        ]
    )
    lifted, sent = {}, {}

    def start_lift(n):
        lifted[n] = rep(order.after(parts[n]), lift)

    def start_across(n):
        owned = down_t if n < CUTS else up
        both = pick_two(
            from_feeder, own_at, feeder_at, owned, order.after(lifted[n]), n % CUTS
        )
        sent[n] = rep(both, across)
        order.arrived(both)

    mine, theirs, halves = {}, {}, {}

    def start_base(chunk):
        while len(pieces[chunk]) < count + 1:
            ring_step(chunk)
        result = product(shards, their_same, halves["their"], pieces[chunk], jnp.bfloat16)
        theirs[chunk] = partner(result)
        order.arrived(result)

    def keep_base(chunk):
        mine[chunk] = product(shards, order.after(tokens), halves["mine"], pieces[chunk], F32)
        order.arrived(mine[chunk])

    lows = {}
    for action in PLAN:
        kind, n = action[0], action[1]
        if kind == "ring":
            ring_step(n)
        elif kind == "ring_done":
            order.arrived(*pieces[n][-2:])
        elif kind == "lift":
            start_lift(n)
        elif kind == "lift_done":
            order.arrived(lifted[n])
        elif kind == "across":
            start_across(n)
        elif kind == "across_done":
            order.arrived(sent[n])
        elif kind == "base_done":
            order.arrived(theirs[n])
        elif kind == "swap_mine":
            halves["mine"] = other_core(order.after(tokens))
        elif kind == "swap_their":
            halves["their"] = other_core(order.after(their_same))
        elif kind == "swap_done":
            order.arrived(halves["mine" if n == 0 else "their"])
        elif kind == "tokens_done":
            order.arrived(their_same)
        elif kind == "low":
            lows["a"] = low_partial(
                table, order.after(tokens), (down_t, [sent[i] for i in range(CUTS)])
            )
            lows["b"] = other_core(lows["a"])
            order.arrived(lows["a"])
        elif kind == "base":
            start_base(n)
        elif kind == "keep":
            keep_base(n)
    chunks = range(len(widths))
    ups = (up, [sent[i] for i in range(CUTS, 2 * CUTS)])
    return finish(
        table,
        live,
        half.reshape(1),
        lows["a"],
        lows["b"],
        [mine[c] for c in chunks],
        [theirs[c] for c in chunks],
        ups,
    )


def solution(mesh):
    in_specs = (
        P(("groups", "replica"), "tensor"),
        P("replica", "tensor"),
        P(("groups", "replica"), "tensor", None),
        P(("groups", "replica"), None, "tensor"),
        P(("groups", "replica")),
        P(("groups", "replica")),
    )
    out_specs = P(("groups", "replica"), "tensor")
    body = functools.partial(local, mesh.shape["groups"], mesh.shape["replica"])
    return jax.shard_map(body, mesh=mesh, in_specs=in_specs, out_specs=out_specs, check_vma=False)
```

```python
import functools

import jax
import jax.numpy as jnp
import numpy as np
from jax import lax
from jax.experimental import pallas as pl
from jax.experimental.pallas import tpu as pltpu
from jax.sharding import PartitionSpec as P

ADAPTER_SCALE = 2.0
F32 = jnp.float32
VMEM_LIMIT = 48 * 1024 * 1024


CUTS = 2
CHUNKS = (5, 3)
PLAN = [
    ("lift", 0),
    ("ring", 0),
    ("swap_mine", 0),
    ("swap_done", 0),
    ("ring_done", 0),
    ("ring", 0),
    ("lift_done", 0),
    ("across", 0),
    ("lift", 1),
    ("ring", 0),
    ("across_done", 0),
    ("lift_done", 1),
    ("across", 1),
    ("ring_done", 0),
    ("swap_their", 0),
    ("tokens_done", 0),
    ("lift", 2),
    ("ring", 1),
    ("ring", 0),
    ("ring_done", 0),
    ("base", 0),
    ("lift_done", 2),
    ("across_done", 1),
    ("across", 2),
    ("lift", 3),
    ("ring_done", 1),
    ("ring_done", 1),
    ("ring", 1),
    ("keep", 0),
    ("low", 0),
    ("lift_done", 3),
    ("across", 3),
    ("across_done", 2),
    ("ring_done", 1),
    ("ring", 1),
    ("ring_done", 1),
    ("ring", 1),
    ("ring_done", 1),
    ("base", 1),
    ("base_done", 0),
    ("base_done", 0),
    ("keep", 1),
]


def routes(count):
    planes = count // 2
    ring = [2 * z for z in range(planes)] + [2 * z + 1 for z in reversed(range(planes))]
    ahead = [(ring[p], ring[(p + 1) % count]) for p in range(count)]
    back = [(b, a) for a, b in ahead]
    across = [(i, i ^ 1) for i in range(count)]
    diagonal = [(i, (i + 1 if i % 2 else i - 1) % count) for i in range(count)]
    lift = [(i, (i + 2 if i % 2 else i - 2) % count) for i in range(count)]
    return ring, ahead, back, across, diagonal, lift


def params(count):
    return pltpu.CompilerParams(
        dimension_semantics=("arbitrary",) * count, vmem_limit_bytes=VMEM_LIMIT
    )


def pick(index, down_t, up, cuts):
    count = index.shape[0]
    _, rank, width = down_t.shape
    part = rank // cuts
    spec = pl.BlockSpec((1, rank, width), lambda i, at: (at[i], 0, 0))
    out = pl.BlockSpec((1, part, width), lambda i, at: (i, 0, 0))

    def body(at, a, b, *outs):
        for n, ref in enumerate(outs):
            source = a if n < cuts else b
            start = (n % cuts) * part
            ref[...] = source[:, start : start + part, :]

    shape = jax.ShapeDtypeStruct((count, part, width), down_t.dtype)
    return pl.pallas_call(
        body,
        grid_spec=pltpu.PrefetchScalarGridSpec(
            num_scalar_prefetch=1,
            grid=(count,),
            in_specs=[spec, spec],
            out_specs=[out] * (2 * cuts),
        ),
        out_shape=[shape] * (2 * cuts),
        compiler_params=params(1),
        cost_estimate=pl.CostEstimate(
            flops=0, bytes_accessed=count * rank * width * 8, transcendentals=0
        ),
    )(index, down_t, up)


def pick_two(which, first, second, a, b, cut):
    count = which.shape[0]
    block = (1,) + b.shape[1:]

    def body(which_ref, first_ref, second_ref, a_ref, b_ref, out_ref):
        side = which_ref[pl.program_id(0)]

        @pl.when(side == 0)
        def _():
            out_ref[...] = a_ref[...]

        @pl.when(side != 0)
        def _():
            out_ref[...] = b_ref[...]

    return pl.pallas_call(
        body,
        grid_spec=pltpu.PrefetchScalarGridSpec(
            num_scalar_prefetch=3,
            grid=(count,),
            in_specs=[
                pl.BlockSpec(block, lambda i, w, f, s: (f[i], cut, 0)),
                pl.BlockSpec(block, lambda i, w, f, s: (s[i], 0, 0)),
            ],
            out_specs=pl.BlockSpec(block, lambda i, w, f, s: (i, 0, 0)),
        ),
        out_shape=jax.ShapeDtypeStruct((count,) + b.shape[1:], b.dtype),
        compiler_params=params(1),
        cost_estimate=pl.CostEstimate(
            flops=0, bytes_accessed=count * int(np.prod(block)) * 6, transcendentals=0
        ),
    )(which, first, second, a, b)


def choose_specs(sources):
    owned, parts = sources
    specs = [pl.BlockSpec((1,) + owned.shape[1:], lambda i, table, *rest: (table[1, i], 0, 0))]
    for p in parts:
        specs.append(
            pl.BlockSpec((1,) + p.shape[1:], lambda i, table, *rest: (table[2, i], 0, 0))
        )
    return specs


def low_partial(table, tokens, sources):
    blocks = table.shape[1]
    rows, width = tokens.shape[0] // blocks, tokens.shape[1]
    rank = sources[0].shape[1]

    def body(table_ref, x_ref, own_ref, *refs):
        place = table_ref[0, pl.program_id(0)]
        out_ref = refs[-1]

        def write(weight):
            out_ref[...] = lax.dot_general(
                x_ref[...], weight, (((1,), (1,)), ((), ())), preferred_element_type=F32
            )

        @pl.when(place == 0)
        def _():
            write(own_ref[0])

        @pl.when(place != 0)
        def _():
            write(jnp.concatenate([r[0] for r in refs[:-1]], axis=0))

    return pl.pallas_call(
        body,
        grid_spec=pltpu.PrefetchScalarGridSpec(
            num_scalar_prefetch=1,
            grid=(blocks,),
            in_specs=[pl.BlockSpec((rows, width), lambda i, s: (i, 0))] + choose_specs(sources),
            out_specs=pl.BlockSpec((rows, rank), lambda i, s: (i, 0)),
        ),
        out_shape=jax.ShapeDtypeStruct((tokens.shape[0], rank), F32),
        compiler_params=params(1),
        cost_estimate=pl.CostEstimate(
            flops=2 * tokens.shape[0] * width * rank,
            bytes_accessed=tokens.size * 2 + 8 * rank * width * 2,
            transcendentals=0,
        ),
    )(table, tokens, sources[0], *sources[1])


def product(shards, same, swapped, pieces, out_type):
    rows, width = same.shape
    columns = pieces[0].shape[1]
    depth = pieces[0].shape[0]
    tile = 256 if rows % 256 == 0 else rows
    count = len(pieces)

    def body(at, same_ref, swapped_ref, *refs):
        x_ref = refs[-1]

        @pl.when(at[count] == 0)
        def _():
            x_ref[:, :width] = same_ref[...]
            x_ref[:, width:] = swapped_ref[...]

        @pl.when(at[count] != 0)
        def _():
            x_ref[:, :width] = swapped_ref[...]
            x_ref[:, width:] = same_ref[...]

        total = None
        for k in range(count):
            x = x_ref[:, pl.ds(pl.multiple_of(at[k], depth), depth)]
            if k == count - 2:
                x = x[:, : depth // 2]
            if k == count - 1:
                x = x[:, depth // 2 :]
            term = jnp.dot(x, refs[k][...], preferred_element_type=F32)
            total = term if total is None else total + term
        refs[count][...] = total.astype(out_type)

    return pl.pallas_call(
        body,
        grid_spec=pltpu.PrefetchScalarGridSpec(
            num_scalar_prefetch=1,
            grid=(rows // tile,),
            in_specs=[pl.BlockSpec((tile, width), lambda i, at: (i, 0))] * 2
            + [pl.BlockSpec(p.shape, lambda i, at: (0, 0)) for p in pieces],
            out_specs=pl.BlockSpec((tile, columns), lambda i, at: (i, 0)),
            scratch_shapes=[pltpu.VMEM((tile, 2 * width), same.dtype)],
        ),
        out_shape=jax.ShapeDtypeStruct((rows, columns), out_type),
        compiler_params=params(1),
        cost_estimate=pl.CostEstimate(
            flops=4 * rows * width * columns,
            bytes_accessed=(2 * rows * width + 2 * width * columns + 2 * rows * columns) * 2,
            transcendentals=0,
        ),
    )(shards, same, swapped, *pieces)


def finish(table, live, half, low_a, low_b, mine, theirs, sources):
    blocks = table.shape[1]
    rows = mine[0].shape[0] // blocks
    widths = [m.shape[1] for m in mine]
    part = sum(widths)
    rank = sources[0].shape[1]
    chunks = len(mine)

    def body(table_ref, live_ref, half_ref, la, lb, *refs):
        out_ref = refs[-1]
        block = pl.program_id(0)
        place = table_ref[0, block]
        low = (la[...] + lb[...]).astype(jnp.bfloat16)
        mine_refs, theirs_refs = refs[:chunks], refs[chunks : 2 * chunks]
        own_ref, part_refs = refs[2 * chunks], refs[2 * chunks + 1 : -1]

        def write(weight_of, left, right):
            start = 0
            for ref in tuple(left) + tuple(right):
                width = ref.shape[1]
                delta = jnp.dot(low, weight_of(start, width), preferred_element_type=F32)
                total = ref[...].astype(F32) + ADAPTER_SCALE * delta
                alive = lax.broadcasted_iota(jnp.int32, (rows, width), 0) < live_ref[block]
                out_ref[:, start : start + width] = jnp.where(alive, total, 0.0).astype(
                    out_ref.dtype
                )
                start += width

        def from_own(start, width):
            return own_ref[0, :, start : start + width]

        def from_parts(start, width):
            return jnp.concatenate([r[0, :, start : start + width] for r in part_refs], axis=0)

        for n, weight_of in enumerate((from_own, from_parts)):
            for side in range(2):

                @pl.when(jnp.logical_and(place == n, half_ref[0] == side))
                def _(weight_of=weight_of, side=side):
                    if side == 0:
                        write(weight_of, mine_refs, theirs_refs)
                    else:
                        write(weight_of, theirs_refs, mine_refs)

    row = lambda width: pl.BlockSpec((rows, width), lambda i, s, l, h: (i, 0))
    return pl.pallas_call(
        body,
        grid_spec=pltpu.PrefetchScalarGridSpec(
            num_scalar_prefetch=3,
            grid=(blocks,),
            in_specs=[row(rank), row(rank)]
            + [row(w) for w in widths + widths]
            + choose_specs(sources),
            out_specs=row(2 * part),
        ),
        out_shape=jax.ShapeDtypeStruct((rows * blocks, 2 * part), jnp.bfloat16),
        compiler_params=params(1),
        cost_estimate=pl.CostEstimate(
            flops=4 * rows * blocks * part * rank,
            bytes_accessed=rows * blocks * part * 10 + 8 * rank * part * 4,
            transcendentals=0,
        ),
    )(table, live, half, low_a, low_b, *mine, *theirs, sources[0], *sources[1])


def ranks(ids, owner_of, owner):
    hit = owner_of == owner
    return hit, jnp.cumsum(hit.astype(jnp.int32)) - hit.astype(jnp.int32)


def slots(ids, per_device, owner, count):
    hit, place = ranks(ids, ids // per_device, owner)
    at = jnp.arange(count)[:, None]
    chosen = jnp.logical_and(hit[None, :], place[None, :] == at)
    return jnp.sum(jnp.where(chosen, (ids % per_device)[None, :], 0), axis=1).astype(jnp.int32)


class Order:
    def __init__(self):
        self.last = ()

    def after(self, x):
        return lax.optimization_barrier((x,) + self.last)[0] if self.last else x

    def arrived(self, *found):
        self.last = (self.last + found)[-6:]


def local(groups, count, tokens, query_matrix, down, up, ids, live):
    ring, ahead, back, across, diagonal, lift = routes(count)
    rep = lambda a, route: lax.ppermute(a, "replica", route)
    partner = lambda a: lax.ppermute(a, "groups", [(i, i ^ 1) for i in range(groups)])
    other_core = lambda a: lax.ppermute(a, "tensor", [(0, 1), (1, 0)])
    order = Order()

    depth, out_half = query_matrix.shape
    quarter = out_half // 2
    blocks = ids.shape[0]
    per_device = down.shape[0]
    most = blocks - 1
    half = (lax.axis_index("groups") % 2).astype(jnp.int32)
    me = lax.axis_index("replica").astype(jnp.int32)
    core = lax.axis_index("tensor").astype(jnp.int32)

    place = np.argsort(ring)
    offsets = np.zeros((count, count + 1), np.int32)
    for r in range(count):
        for step in range(1, count // 2 + 1):
            offsets[r, 2 * step - 1] = ring[(place[r] - step) % count] * depth
            offsets[r, 2 * step] = ring[(place[r] + step) % count] * depth
        offsets[r, 0] = r * depth
    shards = lax.dynamic_index_in_dim(jnp.asarray(offsets), me, 0, keepdims=False)
    shards = jnp.concatenate([shards, core.reshape(1)])

    widths = [quarter * n // 8 for n in CHUNKS]
    starts = [sum(widths[:n]) for n in range(len(widths))]
    pieces = [
        [lax.dynamic_slice(query_matrix, (0, half * quarter + s), (depth, w))]
        for s, w in zip(starts, widths)
    ]

    def ring_step(chunk):
        held = pieces[chunk]
        step = (len(held) + 1) // 2
        low_side, high_side = (held[0], held[0]) if step == 1 else held[-2:]
        if step == count // 2:
            low_side, high_side = low_side[: depth // 2], high_side[depth // 2 :]
        held += [rep(order.after(low_side), ahead), rep(order.after(high_side), back)]

    their_same = partner(tokens)
    ids_across = rep(ids, across)
    ids_diagonal = rep(ids, diagonal)

    down_t = jnp.swapaxes(down, 1, 2)
    parts = pick(slots(ids_diagonal, per_device, me, most), down_t, up, CUTS)
    feeder = jnp.where(me % 2 == 1, me - 2, me + 2) % count
    across_owner = ids_across // per_device
    _, feeder_place = ranks(ids_across, across_owner, feeder)
    from_feeder = (across_owner == feeder).astype(jnp.int32)
    own_at = jnp.where(across_owner == me, ids_across % per_device, 0).astype(jnp.int32)
    feeder_at = jnp.where(from_feeder == 1, jnp.minimum(feeder_place, most - 1), 0).astype(jnp.int32)
    foreign = (ids // per_device != me).astype(jnp.int32)
    table = jnp.stack(
        [
            foreign,
            jnp.where(foreign == 0, ids % per_device, 0).astype(jnp.int32),
            jnp.where(foreign == 1, jnp.arange(blocks, dtype=jnp.int32), 0),
        ]
    )
    lifted, sent = {}, {}

    def start_lift(n):
        lifted[n] = rep(order.after(parts[n]), lift)

    def start_across(n):
        owned = down_t if n < CUTS else up
        both = pick_two(
            from_feeder, own_at, feeder_at, owned, order.after(lifted[n]), n % CUTS
        )
        sent[n] = rep(both, across)
        order.arrived(both)

    mine, theirs, halves = {}, {}, {}

    def start_base(chunk):
        while len(pieces[chunk]) < count + 1:
            ring_step(chunk)
        result = product(shards, their_same, halves["their"], pieces[chunk], jnp.bfloat16)
        theirs[chunk] = partner(result)
        order.arrived(result)

    def keep_base(chunk):
        mine[chunk] = product(shards, order.after(tokens), halves["mine"], pieces[chunk], F32)
        order.arrived(mine[chunk])

    lows = {}
    for action in PLAN:
        kind, n = action[0], action[1]
        if kind == "ring":
            ring_step(n)
        elif kind == "ring_done":
            order.arrived(*pieces[n][-2:])
        elif kind == "lift":
            start_lift(n)
        elif kind == "lift_done":
            order.arrived(lifted[n])
        elif kind == "across":
            start_across(n)
        elif kind == "across_done":
            order.arrived(sent[n])
        elif kind == "base_done":
            order.arrived(theirs[n])
        elif kind == "swap_mine":
            halves["mine"] = other_core(order.after(tokens))
        elif kind == "swap_their":
            halves["their"] = other_core(order.after(their_same))
        elif kind == "swap_done":
            order.arrived(halves["mine" if n == 0 else "their"])
        elif kind == "tokens_done":
            order.arrived(their_same)
        elif kind == "low":
            lows["a"] = low_partial(
                table, order.after(tokens), (down_t, [sent[i] for i in range(CUTS)])
            )
            lows["b"] = other_core(lows["a"])
            order.arrived(lows["a"])
        elif kind == "base":
            start_base(n)
        elif kind == "keep":
            keep_base(n)
    chunks = range(len(widths))
    ups = (up, [sent[i] for i in range(CUTS, 2 * CUTS)])
    return finish(
        table,
        live,
        half.reshape(1),
        lows["a"],
        lows["b"],
        [mine[c] for c in chunks],
        [theirs[c] for c in chunks],
        ups,
    )


def solution(mesh):
    in_specs = (
        P(("groups", "replica"), "tensor"),
        P("replica", "tensor"),
        P(("groups", "replica"), "tensor", None),
        P(("groups", "replica"), None, "tensor"),
        P(("groups", "replica")),
        P(("groups", "replica")),
    )
    out_specs = P(("groups", "replica"), "tensor")
    body = functools.partial(local, mesh.shape["groups"], mesh.shape["replica"])
    return jax.shard_map(body, mesh=mesh, in_specs=in_specs, out_specs=out_specs, check_vma=False)
```

```python
import functools

import jax
import jax.numpy as jnp
import numpy as np
from jax import lax
from jax.experimental import pallas as pl
from jax.experimental.pallas import tpu as pltpu
from jax.sharding import PartitionSpec as P

ADAPTER_SCALE = 2.0
F32 = jnp.float32
VMEM_LIMIT = 48 * 1024 * 1024


CUTS = 2
CHUNKS = (5, 3)
PLAN = [
    ("lift", 0),
    ("ring", 0),
    ("swap_mine", 0),
    ("swap_done", 0),
    ("ring_done", 0),
    ("ring", 0),
    ("across", 0),
    ("lift", 1),
    ("ring", 0),
    ("lift_done", 0),
    ("across_done", 0),
    ("lift_done", 1),
    ("across", 1),
    ("ring_done", 0),
    ("swap_their", 0),
    ("tokens_done", 0),
    ("lift", 2),
    ("ring", 1),
    ("tokens_done", 0),
    ("ring", 0),
    ("ring_done", 0),
    ("base", 0),
    ("across", 2),
    ("ring_done", 1),
    ("ring_done", 1),
    ("lift", 3),
    ("swap_done", 0),
    ("ring", 1),
    ("keep", 0),
    ("swap_done", 1),
    ("low", 0),
    ("ring", 1),
    ("across", 3),
    ("across_done", 2),
    ("swap_done", 1),
    ("ring_done", 1),
    ("lift_done", 3),
    ("ring", 1),
    ("tokens_done", 0),
    ("ring_done", 0),
    ("tokens_done", 0),
    ("ring_done", 1),
    ("base_done", 0),
    ("ring_done", 1),
    ("base", 1),
    ("keep", 1),
]


def routes(count):
    planes = count // 2
    ring = [2 * z for z in range(planes)] + [2 * z + 1 for z in reversed(range(planes))]
    ahead = [(ring[p], ring[(p + 1) % count]) for p in range(count)]
    back = [(b, a) for a, b in ahead]
    across = [(i, i ^ 1) for i in range(count)]
    diagonal = [(i, (i + 1 if i % 2 else i - 1) % count) for i in range(count)]
    lift = [(i, (i + 2 if i % 2 else i - 2) % count) for i in range(count)]
    return ring, ahead, back, across, diagonal, lift


def params(count):
    return pltpu.CompilerParams(
        dimension_semantics=("arbitrary",) * count, vmem_limit_bytes=VMEM_LIMIT
    )


def pick(index, down_t, up, cuts):
    count = index.shape[0]
    _, rank, width = down_t.shape
    part = rank // cuts
    spec = pl.BlockSpec((1, rank, width), lambda i, at: (at[i], 0, 0))
    out = pl.BlockSpec((1, part, width), lambda i, at: (i, 0, 0))

    def body(at, a, b, *outs):
        for n, ref in enumerate(outs):
            source = a if n < cuts else b
            start = (n % cuts) * part
            ref[...] = source[:, start : start + part, :]

    shape = jax.ShapeDtypeStruct((count, part, width), down_t.dtype)
    return pl.pallas_call(
        body,
        grid_spec=pltpu.PrefetchScalarGridSpec(
            num_scalar_prefetch=1,
            grid=(count,),
            in_specs=[spec, spec],
            out_specs=[out] * (2 * cuts),
        ),
        out_shape=[shape] * (2 * cuts),
        compiler_params=params(1),
        cost_estimate=pl.CostEstimate(
            flops=0, bytes_accessed=count * rank * width * 8, transcendentals=0
        ),
    )(index, down_t, up)


def pick_two(which, first, second, a, b, cut):
    count = which.shape[0]
    block = (1,) + b.shape[1:]

    def body(which_ref, first_ref, second_ref, a_ref, b_ref, out_ref):
        side = which_ref[pl.program_id(0)]

        @pl.when(side == 0)
        def _():
            out_ref[...] = a_ref[...]

        @pl.when(side != 0)
        def _():
            out_ref[...] = b_ref[...]

    return pl.pallas_call(
        body,
        grid_spec=pltpu.PrefetchScalarGridSpec(
            num_scalar_prefetch=3,
            grid=(count,),
            in_specs=[
                pl.BlockSpec(block, lambda i, w, f, s: (f[i], cut, 0)),
                pl.BlockSpec(block, lambda i, w, f, s: (s[i], 0, 0)),
            ],
            out_specs=pl.BlockSpec(block, lambda i, w, f, s: (i, 0, 0)),
        ),
        out_shape=jax.ShapeDtypeStruct((count,) + b.shape[1:], b.dtype),
        compiler_params=params(1),
        cost_estimate=pl.CostEstimate(
            flops=0, bytes_accessed=count * int(np.prod(block)) * 6, transcendentals=0
        ),
    )(which, first, second, a, b)


def choose_specs(sources):
    owned, parts = sources
    specs = [pl.BlockSpec((1,) + owned.shape[1:], lambda i, table, *rest: (table[1, i], 0, 0))]
    for p in parts:
        specs.append(
            pl.BlockSpec((1,) + p.shape[1:], lambda i, table, *rest: (table[2, i], 0, 0))
        )
    return specs


def low_partial(table, tokens, sources):
    blocks = table.shape[1]
    rows, width = tokens.shape[0] // blocks, tokens.shape[1]
    rank = sources[0].shape[1]

    def body(table_ref, x_ref, own_ref, *refs):
        place = table_ref[0, pl.program_id(0)]
        out_ref = refs[-1]

        def write(weight):
            out_ref[...] = lax.dot_general(
                x_ref[...], weight, (((1,), (1,)), ((), ())), preferred_element_type=F32
            )

        @pl.when(place == 0)
        def _():
            write(own_ref[0])

        @pl.when(place != 0)
        def _():
            write(jnp.concatenate([r[0] for r in refs[:-1]], axis=0))

    return pl.pallas_call(
        body,
        grid_spec=pltpu.PrefetchScalarGridSpec(
            num_scalar_prefetch=1,
            grid=(blocks,),
            in_specs=[pl.BlockSpec((rows, width), lambda i, s: (i, 0))] + choose_specs(sources),
            out_specs=pl.BlockSpec((rows, rank), lambda i, s: (i, 0)),
        ),
        out_shape=jax.ShapeDtypeStruct((tokens.shape[0], rank), F32),
        compiler_params=params(1),
        cost_estimate=pl.CostEstimate(
            flops=2 * tokens.shape[0] * width * rank,
            bytes_accessed=tokens.size * 2 + 8 * rank * width * 2,
            transcendentals=0,
        ),
    )(table, tokens, sources[0], *sources[1])


def product(shards, same, swapped, pieces, out_type):
    rows, width = same.shape
    columns = pieces[0].shape[1]
    depth = pieces[0].shape[0]
    tile = 256 if rows % 256 == 0 else rows
    count = len(pieces)

    def body(at, same_ref, swapped_ref, *refs):
        x_ref = refs[-1]

        @pl.when(at[count] == 0)
        def _():
            x_ref[:, :width] = same_ref[...]
            x_ref[:, width:] = swapped_ref[...]

        @pl.when(at[count] != 0)
        def _():
            x_ref[:, :width] = swapped_ref[...]
            x_ref[:, width:] = same_ref[...]

        total = None
        for k in range(count):
            x = x_ref[:, pl.ds(pl.multiple_of(at[k], depth), depth)]
            if k == count - 2:
                x = x[:, : depth // 2]
            if k == count - 1:
                x = x[:, depth // 2 :]
            term = jnp.dot(x, refs[k][...], preferred_element_type=F32)
            total = term if total is None else total + term
        refs[count][...] = total.astype(out_type)

    return pl.pallas_call(
        body,
        grid_spec=pltpu.PrefetchScalarGridSpec(
            num_scalar_prefetch=1,
            grid=(rows // tile,),
            in_specs=[pl.BlockSpec((tile, width), lambda i, at: (i, 0))] * 2
            + [pl.BlockSpec(p.shape, lambda i, at: (0, 0)) for p in pieces],
            out_specs=pl.BlockSpec((tile, columns), lambda i, at: (i, 0)),
            scratch_shapes=[pltpu.VMEM((tile, 2 * width), same.dtype)],
        ),
        out_shape=jax.ShapeDtypeStruct((rows, columns), out_type),
        compiler_params=params(1),
        cost_estimate=pl.CostEstimate(
            flops=4 * rows * width * columns,
            bytes_accessed=(2 * rows * width + 2 * width * columns + 2 * rows * columns) * 2,
            transcendentals=0,
        ),
    )(shards, same, swapped, *pieces)


def finish(table, live, half, low_a, low_b, mine, theirs, sources):
    blocks = table.shape[1]
    rows = mine[0].shape[0] // blocks
    widths = [m.shape[1] for m in mine]
    part = sum(widths)
    rank = sources[0].shape[1]
    chunks = len(mine)

    def body(table_ref, live_ref, half_ref, la, lb, *refs):
        out_ref = refs[-1]
        block = pl.program_id(0)
        place = table_ref[0, block]
        low = (la[...] + lb[...]).astype(jnp.bfloat16)
        mine_refs, theirs_refs = refs[:chunks], refs[chunks : 2 * chunks]
        own_ref, part_refs = refs[2 * chunks], refs[2 * chunks + 1 : -1]

        def write(weight_of, left, right):
            start = 0
            for ref in tuple(left) + tuple(right):
                width = ref.shape[1]
                delta = jnp.dot(low, weight_of(start, width), preferred_element_type=F32)
                total = ref[...].astype(F32) + ADAPTER_SCALE * delta
                alive = lax.broadcasted_iota(jnp.int32, (rows, width), 0) < live_ref[block]
                out_ref[:, start : start + width] = jnp.where(alive, total, 0.0).astype(
                    out_ref.dtype
                )
                start += width

        def from_own(start, width):
            return own_ref[0, :, start : start + width]

        def from_parts(start, width):
            return jnp.concatenate([r[0, :, start : start + width] for r in part_refs], axis=0)

        for n, weight_of in enumerate((from_own, from_parts)):
            for side in range(2):

                @pl.when(jnp.logical_and(place == n, half_ref[0] == side))
                def _(weight_of=weight_of, side=side):
                    if side == 0:
                        write(weight_of, mine_refs, theirs_refs)
                    else:
                        write(weight_of, theirs_refs, mine_refs)

    row = lambda width: pl.BlockSpec((rows, width), lambda i, s, l, h: (i, 0))
    return pl.pallas_call(
        body,
        grid_spec=pltpu.PrefetchScalarGridSpec(
            num_scalar_prefetch=3,
            grid=(blocks,),
            in_specs=[row(rank), row(rank)]
            + [row(w) for w in widths + widths]
            + choose_specs(sources),
            out_specs=row(2 * part),
        ),
        out_shape=jax.ShapeDtypeStruct((rows * blocks, 2 * part), jnp.bfloat16),
        compiler_params=params(1),
        cost_estimate=pl.CostEstimate(
            flops=4 * rows * blocks * part * rank,
            bytes_accessed=rows * blocks * part * 10 + 8 * rank * part * 4,
            transcendentals=0,
        ),
    )(table, live, half, low_a, low_b, *mine, *theirs, sources[0], *sources[1])


def ranks(ids, owner_of, owner):
    hit = owner_of == owner
    return hit, jnp.cumsum(hit.astype(jnp.int32)) - hit.astype(jnp.int32)


def slots(ids, per_device, owner, count):
    hit, place = ranks(ids, ids // per_device, owner)
    at = jnp.arange(count)[:, None]
    chosen = jnp.logical_and(hit[None, :], place[None, :] == at)
    return jnp.sum(jnp.where(chosen, (ids % per_device)[None, :], 0), axis=1).astype(jnp.int32)


class Order:
    def __init__(self):
        self.last = ()

    def after(self, x):
        return lax.optimization_barrier((x,) + self.last)[0] if self.last else x

    def arrived(self, *found):
        self.last = (self.last + found)[-6:]


def local(groups, count, tokens, query_matrix, down, up, ids, live):
    ring, ahead, back, across, diagonal, lift = routes(count)
    rep = lambda a, route: lax.ppermute(a, "replica", route)
    partner = lambda a: lax.ppermute(a, "groups", [(i, i ^ 1) for i in range(groups)])
    other_core = lambda a: lax.ppermute(a, "tensor", [(0, 1), (1, 0)])
    order = Order()

    depth, out_half = query_matrix.shape
    quarter = out_half // 2
    blocks = ids.shape[0]
    per_device = down.shape[0]
    most = blocks - 1
    half = (lax.axis_index("groups") % 2).astype(jnp.int32)
    me = lax.axis_index("replica").astype(jnp.int32)
    core = lax.axis_index("tensor").astype(jnp.int32)

    place = np.argsort(ring)
    offsets = np.zeros((count, count + 1), np.int32)
    for r in range(count):
        for step in range(1, count // 2 + 1):
            offsets[r, 2 * step - 1] = ring[(place[r] - step) % count] * depth
            offsets[r, 2 * step] = ring[(place[r] + step) % count] * depth
        offsets[r, 0] = r * depth
    shards = lax.dynamic_index_in_dim(jnp.asarray(offsets), me, 0, keepdims=False)
    shards = jnp.concatenate([shards, core.reshape(1)])

    widths = [quarter * n // 8 for n in CHUNKS]
    starts = [sum(widths[:n]) for n in range(len(widths))]
    pieces = [
        [lax.dynamic_slice(query_matrix, (0, half * quarter + s), (depth, w))]
        for s, w in zip(starts, widths)
    ]

    def ring_step(chunk):
        held = pieces[chunk]
        step = (len(held) + 1) // 2
        low_side, high_side = (held[0], held[0]) if step == 1 else held[-2:]
        if step == count // 2:
            low_side, high_side = low_side[: depth // 2], high_side[depth // 2 :]
        held += [rep(order.after(low_side), ahead), rep(order.after(high_side), back)]

    their_same = partner(tokens)
    ids_across = rep(ids, across)
    ids_diagonal = rep(ids, diagonal)

    down_t = jnp.swapaxes(down, 1, 2)
    parts = pick(slots(ids_diagonal, per_device, me, most), down_t, up, CUTS)
    feeder = jnp.where(me % 2 == 1, me - 2, me + 2) % count
    across_owner = ids_across // per_device
    _, feeder_place = ranks(ids_across, across_owner, feeder)
    from_feeder = (across_owner == feeder).astype(jnp.int32)
    own_at = jnp.where(across_owner == me, ids_across % per_device, 0).astype(jnp.int32)
    feeder_at = jnp.where(from_feeder == 1, jnp.minimum(feeder_place, most - 1), 0).astype(jnp.int32)
    foreign = (ids // per_device != me).astype(jnp.int32)
    table = jnp.stack(
        [
            foreign,
            jnp.where(foreign == 0, ids % per_device, 0).astype(jnp.int32),
            jnp.where(foreign == 1, jnp.arange(blocks, dtype=jnp.int32), 0),
        ]
    )
    lifted, sent = {}, {}

    def start_lift(n):
        lifted[n] = rep(order.after(parts[n]), lift)

    def start_across(n):
        owned = down_t if n < CUTS else up
        both = pick_two(
            from_feeder, own_at, feeder_at, owned, order.after(lifted[n]), n % CUTS
        )
        sent[n] = rep(both, across)
        order.arrived(both)

    mine, theirs, halves = {}, {}, {}

    def start_base(chunk):
        while len(pieces[chunk]) < count + 1:
            ring_step(chunk)
        result = product(shards, their_same, halves["their"], pieces[chunk], jnp.bfloat16)
        theirs[chunk] = partner(result)
        order.arrived(result)

    def keep_base(chunk):
        mine[chunk] = product(shards, order.after(tokens), halves["mine"], pieces[chunk], F32)
        order.arrived(mine[chunk])

    lows = {}
    for action in PLAN:
        kind, n = action[0], action[1]
        if kind == "ring":
            ring_step(n)
        elif kind == "ring_done":
            order.arrived(*pieces[n][-2:])
        elif kind == "lift":
            start_lift(n)
        elif kind == "lift_done":
            order.arrived(lifted[n])
        elif kind == "across":
            start_across(n)
        elif kind == "across_done":
            order.arrived(sent[n])
        elif kind == "base_done":
            order.arrived(theirs[n])
        elif kind == "swap_mine":
            halves["mine"] = other_core(order.after(tokens))
        elif kind == "swap_their":
            halves["their"] = other_core(order.after(their_same))
        elif kind == "swap_done":
            order.arrived(halves["mine" if n == 0 else "their"])
        elif kind == "tokens_done":
            order.arrived(their_same)
        elif kind == "low":
            lows["a"] = low_partial(
                table, order.after(tokens), (down_t, [sent[i] for i in range(CUTS)])
            )
            lows["b"] = other_core(lows["a"])
            order.arrived(lows["a"])
        elif kind == "base":
            start_base(n)
        elif kind == "keep":
            keep_base(n)
    chunks = range(len(widths))
    ups = (up, [sent[i] for i in range(CUTS, 2 * CUTS)])
    return finish(
        table,
        live,
        half.reshape(1),
        lows["a"],
        lows["b"],
        [mine[c] for c in chunks],
        [theirs[c] for c in chunks],
        ups,
    )


def solution(mesh):
    in_specs = (
        P(("groups", "replica"), "tensor"),
        P("replica", "tensor"),
        P(("groups", "replica"), "tensor", None),
        P(("groups", "replica"), None, "tensor"),
        P(("groups", "replica")),
        P(("groups", "replica")),
    )
    out_specs = P(("groups", "replica"), "tensor")
    body = functools.partial(local, mesh.shape["groups"], mesh.shape["replica"])
    return jax.shard_map(body, mesh=mesh, in_specs=in_specs, out_specs=out_specs, check_vma=False)
```

```python
import functools

import jax
import jax.numpy as jnp
import numpy as np
from jax import lax
from jax.experimental import pallas as pl
from jax.experimental.pallas import tpu as pltpu
from jax.sharding import PartitionSpec as P

ADAPTER_SCALE = 2.0
F32 = jnp.float32
VMEM_LIMIT = 48 * 1024 * 1024


CUTS = 2
CHUNKS = (5, 3)
PLAN = [
    ("lift", 0),
    ("ring", 0),
    ("swap_mine", 0),
    ("swap_done", 0),
    ("ring_done", 0),
    ("ring", 0),
    ("across", 0),
    ("lift", 1),
    ("ring", 0),
    ("lift_done", 0),
    ("across_done", 0),
    ("lift_done", 1),
    ("across", 1),
    ("ring_done", 0),
    ("swap_their", 0),
    ("tokens_done", 0),
    ("lift", 2),
    ("ring", 1),
    ("tokens_done", 0),
    ("ring", 0),
    ("ring_done", 0),
    ("base", 0),
    ("across", 2),
    ("ring_done", 1),
    ("ring_done", 1),
    ("lift", 3),
    ("swap_done", 0),
    ("ring", 1),
    ("keep", 0),
    ("swap_done", 1),
    ("low", 0),
    ("ring", 1),
    ("across", 3),
    ("across_done", 2),
    ("swap_done", 1),
    ("ring_done", 1),
    ("lift_done", 3),
    ("ring", 1),
    ("tokens_done", 0),
    ("ring_done", 0),
    ("tokens_done", 0),
    ("ring_done", 1),
    ("base_done", 0),
    ("ring_done", 1),
    ("base", 1),
    ("keep", 1),
]


def routes(count):
    planes = count // 2
    ring = [2 * z for z in range(planes)] + [2 * z + 1 for z in reversed(range(planes))]
    ahead = [(ring[p], ring[(p + 1) % count]) for p in range(count)]
    back = [(b, a) for a, b in ahead]
    across = [(i, i ^ 1) for i in range(count)]
    diagonal = [(i, (i + 1 if i % 2 else i - 1) % count) for i in range(count)]
    lift = [(i, (i + 2 if i % 2 else i - 2) % count) for i in range(count)]
    return ring, ahead, back, across, diagonal, lift


def params(count):
    return pltpu.CompilerParams(
        dimension_semantics=("arbitrary",) * count, vmem_limit_bytes=VMEM_LIMIT
    )


def pick(index, down_t, up, cuts):
    count = index.shape[0]
    _, rank, width = down_t.shape
    part = rank // cuts
    spec = pl.BlockSpec((1, rank, width), lambda i, at: (at[i], 0, 0))
    out = pl.BlockSpec((1, part, width), lambda i, at: (i, 0, 0))

    def body(at, a, b, *outs):
        for n, ref in enumerate(outs):
            source = a if n < cuts else b
            start = (n % cuts) * part
            ref[...] = source[:, start : start + part, :]

    shape = jax.ShapeDtypeStruct((count, part, width), down_t.dtype)
    return pl.pallas_call(
        body,
        grid_spec=pltpu.PrefetchScalarGridSpec(
            num_scalar_prefetch=1,
            grid=(count,),
            in_specs=[spec, spec],
            out_specs=[out] * (2 * cuts),
        ),
        out_shape=[shape] * (2 * cuts),
        compiler_params=params(1),
        cost_estimate=pl.CostEstimate(
            flops=0, bytes_accessed=count * rank * width * 8, transcendentals=0
        ),
    )(index, down_t, up)


def pick_two(which, first, second, a, b, cut):
    count = which.shape[0]
    block = (1,) + b.shape[1:]

    def body(which_ref, first_ref, second_ref, a_ref, b_ref, out_ref):
        side = which_ref[pl.program_id(0)]

        @pl.when(side == 0)
        def _():
            out_ref[...] = a_ref[...]

        @pl.when(side != 0)
        def _():
            out_ref[...] = b_ref[...]

    return pl.pallas_call(
        body,
        grid_spec=pltpu.PrefetchScalarGridSpec(
            num_scalar_prefetch=3,
            grid=(count,),
            in_specs=[
                pl.BlockSpec(block, lambda i, w, f, s: (f[i], cut, 0)),
                pl.BlockSpec(block, lambda i, w, f, s: (s[i], 0, 0)),
            ],
            out_specs=pl.BlockSpec(block, lambda i, w, f, s: (i, 0, 0)),
        ),
        out_shape=jax.ShapeDtypeStruct((count,) + b.shape[1:], b.dtype),
        compiler_params=params(1),
        cost_estimate=pl.CostEstimate(
            flops=0, bytes_accessed=count * int(np.prod(block)) * 6, transcendentals=0
        ),
    )(which, first, second, a, b)


def choose_specs(sources):
    owned, parts = sources
    specs = [pl.BlockSpec((1,) + owned.shape[1:], lambda i, table, *rest: (table[1, i], 0, 0))]
    for p in parts:
        specs.append(
            pl.BlockSpec((1,) + p.shape[1:], lambda i, table, *rest: (table[2, i], 0, 0))
        )
    return specs


def low_partial(table, tokens, sources):
    blocks = table.shape[1]
    rows, width = tokens.shape[0] // blocks, tokens.shape[1]
    rank = sources[0].shape[1]

    def body(table_ref, x_ref, own_ref, *refs):
        place = table_ref[0, pl.program_id(0)]
        out_ref = refs[-1]

        def write(weight):
            out_ref[...] = lax.dot_general(
                x_ref[...], weight, (((1,), (1,)), ((), ())), preferred_element_type=F32
            )

        @pl.when(place == 0)
        def _():
            write(own_ref[0])

        @pl.when(place != 0)
        def _():
            write(jnp.concatenate([r[0] for r in refs[:-1]], axis=0))

    return pl.pallas_call(
        body,
        grid_spec=pltpu.PrefetchScalarGridSpec(
            num_scalar_prefetch=1,
            grid=(blocks,),
            in_specs=[pl.BlockSpec((rows, width), lambda i, s: (i, 0))] + choose_specs(sources),
            out_specs=pl.BlockSpec((rows, rank), lambda i, s: (i, 0)),
        ),
        out_shape=jax.ShapeDtypeStruct((tokens.shape[0], rank), F32),
        compiler_params=params(1),
        cost_estimate=pl.CostEstimate(
            flops=2 * tokens.shape[0] * width * rank,
            bytes_accessed=tokens.size * 2 + 8 * rank * width * 2,
            transcendentals=0,
        ),
    )(table, tokens, sources[0], *sources[1])


def product(shards, same, swapped, pieces, out_type):
    rows, width = same.shape
    columns = pieces[0].shape[1]
    depth = pieces[0].shape[0]
    tile = 256 if rows % 256 == 0 else rows
    count = len(pieces)
    last = shards.shape[0] - 1

    def body(at, same_ref, swapped_ref, *refs):
        x_ref = refs[-1]

        @pl.when(at[last] == 0)
        def _():
            x_ref[:, :width] = same_ref[...]
            x_ref[:, width:] = swapped_ref[...]

        @pl.when(at[last] != 0)
        def _():
            x_ref[:, :width] = swapped_ref[...]
            x_ref[:, width:] = same_ref[...]

        total = None
        for k in range(count):
            x = x_ref[:, pl.ds(pl.multiple_of(at[k], depth), depth)]
            if refs[k].shape[0] < depth:
                x = x[:, : depth // 2] if k == count - 2 else x[:, depth // 2 :]
            term = jnp.dot(x, refs[k][...], preferred_element_type=F32)
            total = term if total is None else total + term
        refs[count][...] = total.astype(out_type)

    return pl.pallas_call(
        body,
        grid_spec=pltpu.PrefetchScalarGridSpec(
            num_scalar_prefetch=1,
            grid=(rows // tile,),
            in_specs=[pl.BlockSpec((tile, width), lambda i, at: (i, 0))] * 2
            + [pl.BlockSpec(p.shape, lambda i, at: (0, 0)) for p in pieces],
            out_specs=pl.BlockSpec((tile, columns), lambda i, at: (i, 0)),
            scratch_shapes=[pltpu.VMEM((tile, 2 * width), same.dtype)],
        ),
        out_shape=jax.ShapeDtypeStruct((rows, columns), out_type),
        compiler_params=params(1),
        cost_estimate=pl.CostEstimate(
            flops=4 * rows * width * columns if count > 7 else 0,
            bytes_accessed=(2 * rows * width + 2 * width * columns + 2 * rows * columns) * 2 if count > 7 else 0,
            transcendentals=0,
        ),
    )(shards, same, swapped, *pieces)


def complete(shards, same, swapped, pieces, partial, out_type):
    rows, width = same.shape
    columns = pieces[0].shape[1]
    depth = 2 * pieces[0].shape[0]
    tile = 256 if rows % 256 == 0 else rows
    last = shards.shape[0] - 1

    def body(at, same_ref, swapped_ref, upper_ref, lower_ref, partial_ref, out_ref):
        def write(x_ref):
            total = partial_ref[...]
            total += jnp.dot(x_ref[:, : depth // 2], upper_ref[...], preferred_element_type=F32)
            total += jnp.dot(x_ref[:, depth // 2 :], lower_ref[...], preferred_element_type=F32)
            out_ref[...] = total.astype(out_type)

        here = at[last - 1] // width == at[last]

        @pl.when(here)
        def _():
            write(same_ref)

        @pl.when(jnp.logical_not(here))
        def _():
            write(swapped_ref)

    column = lambda i, at: (i, (at[last - 1] % width) // depth)
    whole = lambda i, at: (0, 0)
    row = pl.BlockSpec((tile, columns), lambda i, at: (i, 0))
    return pl.pallas_call(
        body,
        grid_spec=pltpu.PrefetchScalarGridSpec(
            num_scalar_prefetch=1,
            grid=(rows // tile,),
            in_specs=[pl.BlockSpec((tile, depth), column)] * 2
            + [pl.BlockSpec(p.shape, whole) for p in pieces]
            + [row],
            out_specs=row,
        ),
        out_shape=jax.ShapeDtypeStruct((rows, columns), out_type),
        compiler_params=params(1),
        cost_estimate=pl.CostEstimate(
            flops=4 * rows * width * columns,
            bytes_accessed=(2 * rows * width + 2 * width * columns + 2 * rows * columns) * 2,
            transcendentals=0,
        ),
    )(shards, same, swapped, *pieces, partial)


def finish(table, live, half, low_a, low_b, mine, theirs, sources):
    blocks = table.shape[1]
    rows = mine[0].shape[0] // blocks
    widths = [m.shape[1] for m in mine]
    part = sum(widths)
    rank = sources[0].shape[1]
    chunks = len(mine)

    def body(table_ref, live_ref, half_ref, la, lb, *refs):
        out_ref = refs[-1]
        block = pl.program_id(0)
        place = table_ref[0, block]
        low = (la[...] + lb[...]).astype(jnp.bfloat16)
        mine_refs, theirs_refs = refs[:chunks], refs[chunks : 2 * chunks]
        own_ref, part_refs = refs[2 * chunks], refs[2 * chunks + 1 : -1]

        def write(weight_of, left, right):
            start = 0
            for ref in tuple(left) + tuple(right):
                width = ref.shape[1]
                delta = jnp.dot(low, weight_of(start, width), preferred_element_type=F32)
                total = ref[...].astype(F32) + ADAPTER_SCALE * delta
                alive = lax.broadcasted_iota(jnp.int32, (rows, width), 0) < live_ref[block]
                out_ref[:, start : start + width] = jnp.where(alive, total, 0.0).astype(
                    out_ref.dtype
                )
                start += width

        def from_own(start, width):
            return own_ref[0, :, start : start + width]

        def from_parts(start, width):
            return jnp.concatenate([r[0, :, start : start + width] for r in part_refs], axis=0)

        for n, weight_of in enumerate((from_own, from_parts)):
            for side in range(2):

                @pl.when(jnp.logical_and(place == n, half_ref[0] == side))
                def _(weight_of=weight_of, side=side):
                    if side == 0:
                        write(weight_of, mine_refs, theirs_refs)
                    else:
                        write(weight_of, theirs_refs, mine_refs)

    row = lambda width: pl.BlockSpec((rows, width), lambda i, s, l, h: (i, 0))
    return pl.pallas_call(
        body,
        grid_spec=pltpu.PrefetchScalarGridSpec(
            num_scalar_prefetch=3,
            grid=(blocks,),
            in_specs=[row(rank), row(rank)]
            + [row(w) for w in widths + widths]
            + choose_specs(sources),
            out_specs=row(2 * part),
        ),
        out_shape=jax.ShapeDtypeStruct((rows * blocks, 2 * part), jnp.bfloat16),
        compiler_params=params(1),
        cost_estimate=pl.CostEstimate(
            flops=4 * rows * blocks * part * rank,
            bytes_accessed=rows * blocks * part * 10 + 8 * rank * part * 4,
            transcendentals=0,
        ),
    )(table, live, half, low_a, low_b, *mine, *theirs, sources[0], *sources[1])


def ranks(ids, owner_of, owner):
    hit = owner_of == owner
    return hit, jnp.cumsum(hit.astype(jnp.int32)) - hit.astype(jnp.int32)


def slots(ids, per_device, owner, count):
    hit, place = ranks(ids, ids // per_device, owner)
    at = jnp.arange(count)[:, None]
    chosen = jnp.logical_and(hit[None, :], place[None, :] == at)
    return jnp.sum(jnp.where(chosen, (ids % per_device)[None, :], 0), axis=1).astype(jnp.int32)


class Order:
    def __init__(self):
        self.last = ()

    def after(self, x):
        return lax.optimization_barrier((x,) + self.last)[0] if self.last else x

    def arrived(self, *found):
        self.last = (self.last + found)[-6:]


def local(groups, count, tokens, query_matrix, down, up, ids, live):
    ring, ahead, back, across, diagonal, lift = routes(count)
    rep = lambda a, route: lax.ppermute(a, "replica", route)
    partner = lambda a: lax.ppermute(a, "groups", [(i, i ^ 1) for i in range(groups)])
    other_core = lambda a: lax.ppermute(a, "tensor", [(0, 1), (1, 0)])
    order = Order()

    depth, out_half = query_matrix.shape
    quarter = out_half // 2
    blocks = ids.shape[0]
    per_device = down.shape[0]
    most = blocks - 1
    half = (lax.axis_index("groups") % 2).astype(jnp.int32)
    me = lax.axis_index("replica").astype(jnp.int32)
    core = lax.axis_index("tensor").astype(jnp.int32)

    place = np.argsort(ring)
    offsets = np.zeros((count, count + 1), np.int32)
    for r in range(count):
        for step in range(1, count // 2 + 1):
            offsets[r, 2 * step - 1] = ring[(place[r] - step) % count] * depth
            offsets[r, 2 * step] = ring[(place[r] + step) % count] * depth
        offsets[r, 0] = r * depth
    shards = lax.dynamic_index_in_dim(jnp.asarray(offsets), me, 0, keepdims=False)
    shards = jnp.concatenate([shards, core.reshape(1)])

    widths = [quarter * n // 8 for n in CHUNKS]
    starts = [sum(widths[:n]) for n in range(len(widths))]
    pieces = [
        [lax.dynamic_slice(query_matrix, (0, half * quarter + s), (depth, w))]
        for s, w in zip(starts, widths)
    ]

    def ring_step(chunk):
        held = pieces[chunk]
        step = (len(held) + 1) // 2
        low_side, high_side = (held[0], held[0]) if step == 1 else held[-2:]
        if step == count // 2:
            low_side, high_side = low_side[: depth // 2], high_side[depth // 2 :]
        held += [rep(order.after(low_side), ahead), rep(order.after(high_side), back)]

    their_same = partner(tokens)
    ids_across = rep(ids, across)
    ids_diagonal = rep(ids, diagonal)

    down_t = jnp.swapaxes(down, 1, 2)
    parts = pick(slots(ids_diagonal, per_device, me, most), down_t, up, CUTS)
    feeder = jnp.where(me % 2 == 1, me - 2, me + 2) % count
    across_owner = ids_across // per_device
    _, feeder_place = ranks(ids_across, across_owner, feeder)
    from_feeder = (across_owner == feeder).astype(jnp.int32)
    own_at = jnp.where(across_owner == me, ids_across % per_device, 0).astype(jnp.int32)
    feeder_at = jnp.where(from_feeder == 1, jnp.minimum(feeder_place, most - 1), 0).astype(jnp.int32)
    foreign = (ids // per_device != me).astype(jnp.int32)
    table = jnp.stack(
        [
            foreign,
            jnp.where(foreign == 0, ids % per_device, 0).astype(jnp.int32),
            jnp.where(foreign == 1, jnp.arange(blocks, dtype=jnp.int32), 0),
        ]
    )
    lifted, sent = {}, {}

    def start_lift(n):
        lifted[n] = rep(order.after(parts[n]), lift)

    def start_across(n):
        owned = down_t if n < CUTS else up
        both = pick_two(
            from_feeder, own_at, feeder_at, owned, order.after(lifted[n]), n % CUTS
        )
        sent[n] = rep(both, across)
        order.arrived(both)

    mine, theirs, halves = {}, {}, {}

    def start_base(chunk):
        while len(pieces[chunk]) < count + 1:
            ring_step(chunk)
        rows_in = (shards, their_same, halves["their"])
        if chunk == len(CHUNKS) - 1:
            partial = product(*rows_in, pieces[chunk][:-2], F32)
            result = complete(*rows_in, pieces[chunk][-2:], partial, jnp.bfloat16)
        else:
            result = product(*rows_in, pieces[chunk], jnp.bfloat16)
        theirs[chunk] = partner(result)
        order.arrived(result)

    def keep_base(chunk):
        mine[chunk] = product(shards, order.after(tokens), halves["mine"], pieces[chunk], F32)
        order.arrived(mine[chunk])

    lows = {}
    for action in PLAN:
        kind, n = action[0], action[1]
        if kind == "ring":
            ring_step(n)
        elif kind == "ring_done":
            order.arrived(*pieces[n][-2:])
        elif kind == "lift":
            start_lift(n)
        elif kind == "lift_done":
            order.arrived(lifted[n])
        elif kind == "across":
            start_across(n)
        elif kind == "across_done":
            order.arrived(sent[n])
        elif kind == "base_done":
            order.arrived(theirs[n])
        elif kind == "swap_mine":
            halves["mine"] = other_core(order.after(tokens))
        elif kind == "swap_their":
            halves["their"] = other_core(order.after(their_same))
        elif kind == "swap_done":
            order.arrived(halves["mine" if n == 0 else "their"])
        elif kind == "tokens_done":
            order.arrived(their_same)
        elif kind == "low":
            lows["a"] = low_partial(
                table, order.after(tokens), (down_t, [sent[i] for i in range(CUTS)])
            )
            lows["b"] = other_core(lows["a"])
            order.arrived(lows["a"])
        elif kind == "base":
            start_base(n)
        elif kind == "keep":
            keep_base(n)
    chunks = range(len(widths))
    ups = (up, [sent[i] for i in range(CUTS, 2 * CUTS)])
    return finish(
        table,
        live,
        half.reshape(1),
        lows["a"],
        lows["b"],
        [mine[c] for c in chunks],
        [theirs[c] for c in chunks],
        ups,
    )


def solution(mesh):
    in_specs = (
        P(("groups", "replica"), "tensor"),
        P("replica", "tensor"),
        P(("groups", "replica"), "tensor", None),
        P(("groups", "replica"), None, "tensor"),
        P(("groups", "replica")),
        P(("groups", "replica")),
    )
    out_specs = P(("groups", "replica"), "tensor")
    body = functools.partial(local, mesh.shape["groups"], mesh.shape["replica"])
    return jax.shard_map(body, mesh=mesh, in_specs=in_specs, out_specs=out_specs, check_vma=False)
```
